32 devices in a mesh: dp: 8 (over z, y), sub: 4 (over x, core).
Axes of the slice: x: 2, y: 2, z: 4, core: 2. Of those that a mesh axis runs over, the one named last changes fastest.
Arguments:
- activations: bfloat16 [6144, 5632], P(('dp', 'sub')), may hold values from -6 to 6
- grad_out: bfloat16 [6144, 1408], P(('dp', 'sub'))
- q_prev: bfloat16 [1408, 32], replicated, may hold values from -0.15625 to 0.15625
Outputs:
- grad_approx: float32 [5632, 1408], P('sub')
- q_new: float32 [1408, 32], replicated
The draws below stay inside these ranges and needn't reach their ends.
All inputs are finite; a program needn't handle non-finite values.
Results may differ from the reference program's by a relative error of at most 0.0036.
Values may be sent and summed in bfloat16 or wider, within the bound.
A program may use at most 64 MiB of HBM per device.

```python
import math
import jax
import jax.numpy as jnp
from jax import lax

C = 1408
FF = 5632
R = 32
TOK_DEV = 192
TOKENS = 6144
N_DP = 8
N_SUB = 4


def draw_grad_out(key, part):
    first = jax.random.fold_in(key, 0)
    place = jnp.arange(TOKENS, dtype=jnp.float32) / TOKENS
    rising = jnp.exp(place * math.log(10.0))[:, None]
    values = jnp.clip(jax.random.normal(first, (TOKENS, C), jnp.float32), -6.0, 6.0) * rising
    return values.astype(jnp.bfloat16)


def level_of(stream_key, shape, shards, low, top_value):
    def one(position, blocks):
        steps = jax.random.uniform(jax.random.fold_in(jax.random.fold_in(stream_key, 6), position), (blocks,), jnp.float32, low / len(shards), top_value / len(shards))
        return jnp.repeat(jnp.exp(steps), shape[position] // blocks).reshape((-1,) + (1,) * (len(shape) - position - 1))

    gain = one(*shards[0])
    for cut in shards[1:]:
        gain = gain * one(*cut)
    return gain


def centred(own_key, shape, deviation, most, shards=(), held_as=jnp.bfloat16):
    gain = level_of(own_key, shape, shards, -0.22, 0.18) if shards else 1.0
    values = jax.random.normal(own_key, shape, jnp.float32) * deviation * gain
    return jnp.minimum(jnp.maximum(values, -most), most).astype(held_as)


def setup_inputs(seed: int = 0) -> dict:
    keys = jax.random.split(jax.random.key(seed), 4)
    return {
        "activations": centred(keys[0], (TOKENS, FF), 1.0, 6.0, ((0, 32),)),
        "grad_out": draw_grad_out(jax.random.fold_in(keys[3], 71), 0),
        "q_prev": centred(keys[2], (C, R), C ** -0.5, 0.15625),
    }


def reference(activations, grad_out, q_prev):
    count = N_DP * N_SUB
    act_blocks = activations.reshape(count, TOK_DEV, FF)
    out_blocks = grad_out.reshape(count, TOK_DEV, C)

    def left_step(total, pair):
        act_block, out_block = pair
        u_part = jnp.dot(out_block.astype(jnp.float32), q_prev.astype(jnp.float32), preferred_element_type=jnp.float32).astype(jnp.bfloat16)
        return (total + jnp.dot(act_block.T.astype(jnp.float32), u_part.astype(jnp.float32), preferred_element_type=jnp.float32), None)
    p_sum, _ = lax.scan(left_step, jnp.zeros((FF, R), jnp.float32), (act_blocks, out_blocks))
    gram = jnp.dot(p_sum.T, p_sum, precision=lax.Precision.HIGHEST)
    lower = lax.linalg.cholesky(gram)
    p_hat = lax.linalg.triangular_solve(lower, p_sum, left_side=False, lower=True, transpose_a=True)
    p_low = p_hat.astype(jnp.bfloat16)

    def right_step(total, pair):
        act_block, out_block = pair
        v_part = jnp.dot(act_block.astype(jnp.float32), p_low.astype(jnp.float32), preferred_element_type=jnp.float32).astype(jnp.bfloat16)
        return (total + jnp.dot(out_block.T.astype(jnp.float32), v_part.astype(jnp.float32), preferred_element_type=jnp.float32), None)
    q_sum, _ = lax.scan(right_step, jnp.zeros((C, R), jnp.float32), (act_blocks, out_blocks))
    q_new = q_sum / count
    grad_approx = jnp.dot(p_hat, q_new.T, precision=lax.Precision.HIGHEST)
    return (grad_approx, q_new)
```

```python
import functools

import jax
import jax.numpy as jnp
from jax import lax
from jax.experimental import pallas as pl
from jax.experimental.pallas import tpu as pltpu
from jax.sharding import PartitionSpec as P

MESH = pl.DeviceIdType.MESH
F32 = jnp.float32
BF16 = jnp.bfloat16
HIGHEST = lax.Precision.HIGHEST
LANES = 128
HALF = 16


def dot(a, b, dims=((1,), (0,)), precision=None):
    return lax.dot_general(a, b, (dims, ((), ())), precision=precision, preferred_element_type=F32)


def inverse_factor(gram):
    rank = gram.shape[0]
    row = lax.broadcasted_iota(jnp.int32, (rank, rank), 0)
    column = lax.broadcasted_iota(jnp.int32, (rank, rank), 1)
    row2 = lax.broadcasted_iota(jnp.int32, (rank, 2 * rank), 0)
    work = jnp.concatenate([gram, jnp.where(row == column, 1.0, 0.0).astype(F32)], axis=1)
    for j in range(rank):
        scale = lax.rsqrt(work[j : j + 1, j : j + 1])
        pivot = work[j : j + 1, :] * scale
        factor = work[:, j : j + 1] * scale
        work = jnp.where(row2 > j, work - factor * pivot, jnp.where(row2 == j, pivot, work))
    return work[:, rank:]


def split(x):
    high = x.astype(BF16)
    return high, (x - high.astype(F32)).astype(BF16)


def factors_kernel(
    n_dp, n_sub, a_ref, g_ref, q_ref, left_ref, q_out_ref,
    s1_send, s1_recv, part, s2_recv, whole, grams, blocks, q_local, q_recv,
    s1_s, s1_r, s2_s, s2_r, g2_s, g2_r, gm_s, gm_r, b_s, b_r, qs_s, qs_r, qg_s, qg_r,
):
    dp, sub = lax.axis_index("dp"), lax.axis_index("sub")
    n = n_dp * n_sub
    me = dp * n_sub + sub
    block = a_ref.shape[1] // n_sub
    rank = q_ref.shape[1]
    width = part.shape[1] // (n_dp // 2)
    units = 2 * (g_ref.shape[1] // LANES)

    def device(flat):
        return (flat // n_sub, flat % n_sub)

    def piece(ref, owner):
        return ref.at[pl.ds(pl.multiple_of((owner % 2) * HALF, HALF), HALF),
                      pl.ds(pl.multiple_of((owner // 2) * width, LANES), width)]

    def unit(ref, owner):
        return ref.at[pl.ds(pl.multiple_of((owner % 2) * HALF, HALF), HALF),
                      pl.ds(pl.multiple_of((owner // 2) * LANES, LANES), LANES)]

    def columns(s):
        return a_ref[:, pl.ds(pl.multiple_of(s * block, LANES), block)]

    def send(src, dst, s, r, to):
        return pltpu.make_async_remote_copy(
            src_ref=src, dst_ref=dst, send_sem=s, recv_sem=r, device_id=to, device_id_type=MESH)

    barrier = pltpu.get_barrier_semaphore()

    def greet(k, carry):
        pl.semaphore_signal(barrier, inc=1, device_id=device((me + k) % n), device_id_type=MESH)
        return carry

    lax.fori_loop(1, n, greet, 0)

    u = dot(g_ref[...], q_ref[...]).astype(BF16)
    first = []
    for k in range(1, n_sub):
        s = (sub + k) % n_sub
        s1_send[k - 1] = dot(u, columns(s), ((0,), (0,))).astype(BF16)
        if k == 1:
            pl.semaphore_wait(barrier, n - 1)
        copy = send(s1_send.at[k - 1], s1_recv.at[k - 1], s1_s.at[k - 1], s1_r.at[k - 1], (dp, s))
        copy.start()
        first.append(copy)
    total = dot(u, columns(sub), ((0,), (0,)))
    for k in range(1, n_sub):
        first[k - 1].wait_recv()
        total = total + s1_recv[k - 1].astype(F32)
    part[:, pl.ds(0, block)] = total
    if part.shape[1] > block:
        part[:, pl.ds(block, part.shape[1] - block)] = jnp.zeros((rank, part.shape[1] - block), F32)

    second = []
    for k in range(1, n_dp):
        t = (dp + k) % n_dp
        copy = send(piece(part, t), s2_recv.at[k - 1], s2_s.at[k - 1], s2_r.at[k - 1], (t, sub))
        copy.start()
        second.append(copy)
    mine = piece(part, dp)[...]
    for k in range(1, n_dp):
        second[k - 1].wait_recv()
        mine = mine + s2_recv[k - 1]
    piece(whole, dp)[...] = mine
    third = []
    for k in range(1, n_dp):
        t = (dp + k) % n_dp
        copy = send(piece(whole, dp), piece(whole, dp), g2_s.at[k - 1], g2_r.at[k - 1], (t, sub))
        copy.start()
        third.append(copy)
    for k in range(1, n_dp):
        other = (dp + n_dp - k) % n_dp
        send(piece(whole, other), piece(whole, other), g2_s.at[k - 1], g2_r.at[k - 1], (other, sub)).wait_recv()

    p = whole[:, pl.ds(0, block)]
    blocks[sub] = p.astype(BF16)
    gram = dot(p, p, ((1,), (1,)), HIGHEST)
    grams[sub] = jnp.concatenate([gram, jnp.zeros((rank, LANES - rank), F32)], axis=1)
    fourth = []
    for k in range(1, n_sub):
        s = (sub + k) % n_sub
        copy = send(grams.at[sub], grams.at[sub], gm_s.at[k - 1], gm_r.at[k - 1], (dp, s))
        copy.start()
        fourth.append(copy)
    for k in range(1, n_sub):
        s = (sub + k) % n_sub
        copy = send(blocks.at[sub], blocks.at[sub], b_s.at[k - 1], b_r.at[k - 1], (dp, s))
        copy.start()
        fourth.append(copy)
    v = dot(blocks[sub], columns(sub), ((1,), (1,)))
    for k in range(1, n_sub):
        s = (sub + n_sub - k) % n_sub
        send(grams.at[s], grams.at[s], gm_s.at[k - 1], gm_r.at[k - 1], (dp, s)).wait_recv()
    gram = grams[0]
    for s in range(1, n_sub):
        gram = gram + grams[s]
    inverse = inverse_factor(gram[:, :rank])
    high, low = split(dot(inverse, p, precision=HIGHEST))
    left_ref[pl.ds(0, rank), :] = high
    left_ref[pl.ds(rank, rank), :] = high
    left_ref[pl.ds(2 * rank, rank), :] = low

    for k in range(1, n_sub):
        s = (sub + n_sub - k) % n_sub
        send(blocks.at[s], blocks.at[s], b_s.at[k - 1], b_r.at[k - 1], (dp, s)).wait_recv()
        v = v + dot(blocks[s], columns(s), ((1,), (1,)))
    v_low = dot(inverse, v, precision=HIGHEST).astype(BF16)
    q_local[...] = dot(v_low, g_ref[...])

    def scatter(k, carry):
        t = (me + k) % n

        @pl.when(t < units)
        def _():
            send(unit(q_local, t), q_recv.at[k - 1], qs_s.at[k - 1], qs_r.at[k - 1], device(t)).start()

        return carry

    lax.fori_loop(1, n, scatter, 0)

    @pl.when(me < units)
    def _():
        def add(k, total):
            send(unit(q_local, me), q_recv.at[k - 1], qs_s.at[k - 1], qs_r.at[k - 1], device((me + k) % n)).wait_recv()
            return total + q_recv[k - 1]

        total = lax.fori_loop(1, n, add, unit(q_local, me)[...])
        unit(q_out_ref, me)[...] = total * (1.0 / n)

        def spread(k, carry):
            send(unit(q_out_ref, me), unit(q_out_ref, me), qg_s.at[k - 1], qg_r.at[me], device((me + k) % n)).start()
            return carry

        lax.fori_loop(1, n, spread, 0)

    def collect(k, carry):
        t = (me + n - k) % n

        @pl.when(t < units)
        def _():
            send(unit(q_out_ref, t), unit(q_out_ref, t), qg_s.at[k - 1], qg_r.at[t], device(t)).wait_recv()

        return carry

    lax.fori_loop(1, n, collect, 0)

    for copy in first + second + third + fourth:
        copy.wait_send()

    def drain(k, carry):
        t = (me + k) % n

        @pl.when(t < units)
        def _():
            send(unit(q_local, t), q_recv.at[k - 1], qs_s.at[k - 1], qs_r.at[k - 1], device(t)).wait_send()

        @pl.when(me < units)
        def _():
            send(unit(q_out_ref, me), unit(q_out_ref, me), qg_s.at[k - 1], qg_r.at[me], device(t)).wait_send()

        return carry

    lax.fori_loop(1, n, drain, 0)


def result_kernel(left_ref, q_ref, grad_ref, q_new_ref, right):
    rank = q_ref.shape[0]

    @pl.when(pl.program_id(0) == 0)
    def _():
        high, low = split(q_ref[...])
        right[pl.ds(0, rank), :] = high
        right[pl.ds(rank, rank), :] = low
        right[pl.ds(2 * rank, rank), :] = high
        q_new_ref[...] = q_ref[...].T

    grad_ref[...] = dot(left_ref[...], right[...], ((0,), (0,)))


def fast(n_dp, n_sub, activations, grad_out, q_prev):
    hidden, channels, rank = activations.shape[1], grad_out.shape[1], q_prev.shape[1]
    block = hidden // n_sub
    groups = n_dp // 2
    width = -(-(block // LANES) // groups) * LANES
    n = n_dp * n_sub
    dma = pltpu.SemaphoreType.DMA
    vmem = pl.BlockSpec(memory_space=pltpu.VMEM)
    left, q_t = pl.pallas_call(
        functools.partial(factors_kernel, n_dp, n_sub),
        out_shape=(
            jax.ShapeDtypeStruct((3 * rank, block), BF16),
            jax.ShapeDtypeStruct((rank, channels), F32),
        ),
        in_specs=[vmem] * 3,
        out_specs=(vmem, vmem),
        scratch_shapes=[
            pltpu.VMEM((n_sub - 1, rank, block), BF16),
            pltpu.VMEM((n_sub - 1, rank, block), BF16),
            pltpu.VMEM((rank, groups * width), F32),
            pltpu.VMEM((n_dp - 1, HALF, width), F32),
            pltpu.VMEM((rank, groups * width), F32),
            pltpu.VMEM((n_sub, rank, LANES), F32),
            pltpu.VMEM((n_sub, rank, block), BF16),
            pltpu.VMEM((rank, channels), F32),
            pltpu.VMEM((n - 1, HALF, LANES), F32),
            dma((n_sub - 1,)), dma((n_sub - 1,)),
            dma((n_dp - 1,)), dma((n_dp - 1,)),
            dma((n_dp - 1,)), dma((n_dp - 1,)),
            dma((n_sub - 1,)), dma((n_sub - 1,)),
            dma((n_sub - 1,)), dma((n_sub - 1,)),
            dma((n - 1,)), dma((n - 1,)),
            dma((n - 1,)), dma((n,)),
        ],
        compiler_params=pltpu.CompilerParams(
            collective_id=0, has_side_effects=True, vmem_limit_bytes=32 * 2**20
        ),
        name="factors",
    )(activations, grad_out, q_prev)
    return pl.pallas_call(
        result_kernel,
        grid=(block // LANES,),
        out_shape=(
            jax.ShapeDtypeStruct((block, channels), F32),
            jax.ShapeDtypeStruct((channels, rank), F32),
        ),
        in_specs=[
            pl.BlockSpec((3 * rank, LANES), lambda i: (0, i)),
            pl.BlockSpec((rank, channels), lambda i: (0, 0)),
        ],
        out_specs=(
            pl.BlockSpec((LANES, channels), lambda i: (i, 0)),
            pl.BlockSpec((channels, rank), lambda i: (0, 0)),
        ),
        scratch_shapes=[pltpu.VMEM((3 * rank, channels), BF16)],
        compiler_params=pltpu.CompilerParams(vmem_limit_bytes=32 * 2**20),
        name="result",
    )(left, q_t)


def general(activations, grad_out, q_prev):
    u_low = jnp.dot(grad_out, q_prev, preferred_element_type=F32).astype(BF16)
    p_local = jnp.einsum("tf,tr->fr", activations, u_low, preferred_element_type=F32)
    block_rows = activations.shape[1] // lax.axis_size("sub")
    p_sum = lax.psum(p_local, ("dp", "sub"))
    gram = jnp.dot(p_sum.T, p_sum, precision=HIGHEST)
    lower = lax.linalg.cholesky(gram)
    p_hat = lax.linalg.triangular_solve(lower, p_sum, left_side=False, lower=True, transpose_a=True)
    p_low = p_hat.astype(BF16)
    my_hat = lax.dynamic_slice_in_dim(p_hat, lax.axis_index("sub") * block_rows, block_rows, 0)
    v_low = jnp.dot(activations, p_low, preferred_element_type=F32).astype(BF16)
    q_local = jnp.einsum("tc,tr->cr", grad_out, v_low, preferred_element_type=F32)
    q_sum = lax.psum(q_local, ("dp", "sub"))
    q_new = q_sum / (lax.axis_size("dp") * lax.axis_size("sub"))
    grad_approx = jnp.dot(my_hat, q_new.T, precision=HIGHEST)
    return (grad_approx, q_new)


def solution(mesh):
    n_dp, n_sub = mesh.shape["dp"], mesh.shape["sub"]

    def per_device(activations, grad_out, q_prev):
        hidden, channels, rank = activations.shape[1], grad_out.shape[1], q_prev.shape[1]
        fits = (
            n_dp % 2 == 0
            and n_sub > 1
            and rank == 2 * HALF
            and hidden % (n_sub * LANES) == 0
            and channels % LANES == 0
            and 2 * channels // LANES <= n_dp * n_sub
        )
        if fits:
            return fast(n_dp, n_sub, activations, grad_out, q_prev)
        return general(activations, grad_out, q_prev)

    return jax.shard_map(
        per_device,
        mesh=mesh,
        in_specs=(P(("dp", "sub"), None), P(("dp", "sub"), None), P()),
        out_specs=(P("sub", None), P()),
        check_vma=False,
    )
```

```python
import functools

import jax
import jax.numpy as jnp
from jax import lax
from jax.experimental import pallas as pl
from jax.experimental.pallas import tpu as pltpu
from jax.sharding import PartitionSpec as P

MESH = pl.DeviceIdType.MESH
F32 = jnp.float32
BF16 = jnp.bfloat16
HIGHEST = lax.Precision.HIGHEST
LANES = 128
HALF = 16
ROWS = 256
HBM = pltpu.MemorySpace.HBM


def dot(a, b, dims=((1,), (0,)), precision=None):
    return lax.dot_general(a, b, (dims, ((), ())), precision=precision, preferred_element_type=F32)


def inverse_factor(gram):
    rank = gram.shape[0]
    row = lax.broadcasted_iota(jnp.int32, (rank, rank), 0)
    column = lax.broadcasted_iota(jnp.int32, (rank, rank), 1)
    row2 = lax.broadcasted_iota(jnp.int32, (rank, 2 * rank), 0)
    work = jnp.concatenate([gram, jnp.where(row == column, 1.0, 0.0).astype(F32)], axis=1)
    for j in range(rank):
        scale = lax.rsqrt(work[j : j + 1, j : j + 1])
        pivot = work[j : j + 1, :] * scale
        factor = work[:, j : j + 1] * scale
        work = jnp.where(row2 > j, work - factor * pivot, jnp.where(row2 == j, pivot, work))
    return work[:, rank:]


def split(x):
    high = x.astype(BF16)
    return high, (x - high.astype(F32)).astype(BF16)


def dot_split(a, b):
    a_high, a_low = split(a)
    b_high, b_low = split(b)
    return dot(jnp.concatenate([a_high, a_high, a_low], 1), jnp.concatenate([b_high, b_low, b_high], 0))


def factors_kernel(
    n_dp, n_sub, a_hbm, g_hbm, q_hbm, left_ref, q_all,
    a_ref, g_ref, q_ref, s1_send, s1_recv, part, part_low, s2_recv, whole_high, whole_low, grams, blocks,
    q_local, q_send, qa_recv, q_parts,
    in_s, a_s, s1_s, s1_r, s2_s, s2_r, gh_s, gh_r, gl_s, gl_r, gm_s, gm_r, b_s, b_r,
    qa_s, qa_r, qb_s, qb_r, qc_s, qc_r,
):
    dp, sub = lax.axis_index("dp"), lax.axis_index("sub")
    n = n_dp * n_sub
    block = a_ref.shape[1] // n_sub
    rank, channels = q_ref.shape
    width = part.shape[1] // (n_dp // 2)
    q_width = q_all.shape[1] // (n_dp // 2)
    dp_to = [None] + [(dp + k) % n_dp for k in range(1, n_dp)]
    dp_from = [None] + [(dp + n_dp - k) % n_dp for k in range(1, n_dp)]
    sub_to = [sub] + [(sub + k) % n_sub for k in range(1, n_sub)]
    sub_from = [sub] + [(sub + n_sub - k) % n_sub for k in range(1, n_sub)]

    def piece(ref, owner, wide):
        return ref.at[pl.ds(pl.multiple_of((owner % 2) * HALF, HALF), HALF),
                      pl.ds(pl.multiple_of((owner // 2) * wide, LANES), wide)]

    def columns(ref, s, wide):
        return ref.at[:, pl.ds(pl.multiple_of(s * wide, LANES), wide)]

    def send(src, dst, s, r, to):
        return pltpu.make_async_remote_copy(
            src_ref=src, dst_ref=dst, send_sem=s, recv_sem=r, device_id=to, device_id_type=MESH)

    sent = []

    def start(*copy):
        copy = send(*copy)
        copy.start()
        sent.append(copy)

    barrier = pltpu.get_barrier_semaphore()
    for k in range(1, n_sub):
        pl.semaphore_signal(barrier, inc=1, device_id=(dp, sub_to[k]), device_id_type=MESH)
    for k in range(1, n_dp):
        pl.semaphore_signal(barrier, inc=1, device_id=(dp_to[k], sub), device_id_type=MESH)

    load_g = pltpu.make_async_copy(g_hbm, g_ref, in_s.at[0])
    load_q = pltpu.make_async_copy(q_hbm, q_ref, in_s.at[1])
    load_g.start()
    load_q.start()
    loads = []
    for k in list(range(1, n_sub)) + [0]:
        load = pltpu.make_async_copy(columns(a_hbm, sub_to[k], block), columns(a_ref, sub_to[k], block), a_s.at[k])
        load.start()
        loads.append(load)
    load_g.wait()
    load_q.wait()
    u = dot(q_ref[...], g_ref[...], ((1,), (1,))).astype(BF16)
    for k in range(1, n_sub):
        loads[k - 1].wait()
        s1_send[k - 1] = dot(u, columns(a_ref, sub_to[k], block)[...]).astype(BF16)
        if k == 1:
            pl.semaphore_wait(barrier, n_sub + n_dp - 2)
        start(s1_send.at[k - 1], s1_recv.at[k - 1], s1_s.at[k - 1], s1_r.at[k - 1], (dp, sub_to[k]))
    loads[n_sub - 1].wait()
    total = dot(u, columns(a_ref, sub, block)[...])
    for k in range(1, n_sub):
        send(s1_send.at[k - 1], s1_recv.at[k - 1], s1_s.at[k - 1], s1_r.at[k - 1], (dp, sub_to[k])).wait_recv()
        total = total + s1_recv[k - 1].astype(F32)
    part[:, pl.ds(0, block)] = total
    part_low[:, pl.ds(0, block)] = total.astype(BF16)
    if part.shape[1] > block:
        rest = part.shape[1] - block
        part[:, pl.ds(block, rest)] = jnp.zeros((rank, rest), F32)
        part_low[:, pl.ds(block, rest)] = jnp.zeros((rank, rest), BF16)

    for k in range(1, n_dp):
        start(piece(part_low, dp_to[k], width), s2_recv.at[k - 1], s2_s.at[k - 1], s2_r.at[k - 1], (dp_to[k], sub))
    mine = piece(part, dp, width)[...]
    for k in range(1, n_dp):
        send(piece(part_low, dp_to[k], width), s2_recv.at[k - 1], s2_s.at[k - 1], s2_r.at[k - 1], (dp_to[k], sub)).wait_recv()
        mine = mine + s2_recv[k - 1].astype(F32)
    high, low = split(mine)
    high_piece, low_piece = piece(whole_high, dp, width), piece(whole_low, dp, width)
    high_piece[...] = high
    low_piece[...] = low
    for k in range(1, n_dp):
        start(high_piece, high_piece, gh_s.at[k - 1], gh_r.at[k - 1], (dp_to[k], sub))
    for k in range(1, n_dp):
        other = piece(whole_high, dp_from[k], width)
        send(other, other, gh_s.at[k - 1], gh_r.at[k - 1], (dp_from[k], sub)).wait_recv()

    p_high = whole_high[:, pl.ds(0, block)]
    gram = dot(p_high, p_high, ((1,), (1,)))
    grams[sub] = jnp.concatenate([gram, jnp.zeros((rank, LANES - rank), F32)], axis=1)
    for k in range(1, n_sub):
        start(grams.at[sub], grams.at[sub], gm_s.at[k - 1], gm_r.at[k - 1], (dp, sub_to[k]))
    for k in range(1, n_sub):
        start(whole_high.at[:, pl.ds(0, block)], blocks.at[sub], b_s.at[k - 1], b_r.at[k - 1], (dp, sub_to[k]))
    for k in range(1, n_dp):
        start(low_piece, low_piece, gl_s.at[k - 1], gl_r.at[k - 1], (dp_to[k], sub))
    v = dot(p_high, columns(a_ref, sub, block)[...], ((1,), (1,)))
    for k in range(1, n_sub):
        other = grams.at[sub_from[k]]
        send(other, other, gm_s.at[k - 1], gm_r.at[k - 1], (dp, sub_from[k])).wait_recv()
    gram = grams[0]
    for s in range(1, n_sub):
        gram = gram + grams[s]
    inverse = inverse_factor(gram[:, :rank])

    for k in range(1, n_sub):
        other = blocks.at[sub_from[k]]
        send(other, other, b_s.at[k - 1], b_r.at[k - 1], (dp, sub_from[k])).wait_recv()
        v = v + dot(other[...], columns(a_ref, sub_from[k], block)[...], ((1,), (1,)))
    v_low = dot_split(inverse, v).astype(BF16)
    q = dot(v_low, g_ref[...])
    rest = q_all.shape[1] - channels
    if rest:
        q = jnp.concatenate([q, jnp.zeros((rank, rest), F32)], axis=1)
    q_local[...] = q
    q_send[...] = q.astype(BF16)
    for k in range(1, n_dp):
        start(piece(q_send, dp_to[k], q_width), qa_recv.at[k - 1], qa_s.at[k - 1], qa_r.at[k - 1], (dp_to[k], sub))

    for k in range(1, n_dp):
        other = piece(whole_low, dp_from[k], width)
        send(other, other, gl_s.at[k - 1], gl_r.at[k - 1], (dp_from[k], sub)).wait_recv()
    p = p_high.astype(F32) + whole_low[:, pl.ds(0, block)].astype(F32)
    high, low = split(dot_split(inverse, p))
    left_ref[pl.ds(0, rank), :] = high
    left_ref[pl.ds(rank, rank), :] = high
    left_ref[pl.ds(2 * rank, rank), :] = low

    total = piece(q_local, dp, q_width)[...]
    for k in range(1, n_dp):
        send(piece(q_send, dp_to[k], q_width), qa_recv.at[k - 1], qa_s.at[k - 1], qa_r.at[k - 1], (dp_to[k], sub)).wait_recv()
        total = total + qa_recv[k - 1].astype(F32)
    q_parts[sub] = total
    for k in range(1, n_sub):
        start(q_parts.at[sub], q_parts.at[sub], qb_s.at[k - 1], qb_r.at[k - 1], (dp, sub_to[k]))
    for k in range(1, n_sub):
        other = q_parts.at[sub_from[k]]
        send(other, other, qb_s.at[k - 1], qb_r.at[k - 1], (dp, sub_from[k])).wait_recv()
    total = q_parts[0]
    for s in range(1, n_sub):
        total = total + q_parts[s]
    mine = piece(q_all, dp, q_width)
    mine[...] = total * (1.0 / n)
    for k in range(1, n_dp):
        start(mine, mine, qc_s.at[k - 1], qc_r.at[k - 1], (dp_to[k], sub))
    for k in range(1, n_dp):
        other = piece(q_all, dp_from[k], q_width)
        send(other, other, qc_s.at[k - 1], qc_r.at[k - 1], (dp_from[k], sub)).wait_recv()

    for copy in sent:
        copy.wait_send()


def result_kernel(left_hbm, q_hbm, grad_ref, q_new_ref, left_ref, q_ref, right, held, in_s, q_s, out_s):
    rank, channels = q_new_ref.shape
    load_q = pltpu.make_async_copy(q_hbm, q_ref, in_s.at[0])
    load_left = pltpu.make_async_copy(left_hbm, left_ref, in_s.at[1])
    load_q.start()
    load_left.start()
    load_q.wait()
    copies = [pltpu.make_async_copy(q_ref.at[:, pl.ds(0, channels)], q_new_ref, q_s)]
    copies[0].start()
    high, low = split(q_ref[:, pl.ds(0, channels)])
    right[pl.ds(0, rank), :] = high
    right[pl.ds(rank, rank), :] = low
    right[pl.ds(2 * rank, rank), :] = high
    load_left.wait()
    rows = grad_ref.shape[0]
    for i, at in enumerate(range(0, rows, ROWS)):
        here = pl.ds(at, min(ROWS, rows - at))
        held[here, :] = dot(left_ref[:, here], right[...], ((0,), (0,)))
        copies.append(pltpu.make_async_copy(held.at[here], grad_ref.at[here], out_s.at[i]))
        copies[-1].start()
    for copy in copies:
        copy.wait()


def widths(n_dp, n_sub, hidden, channels):
    def share(size, parts):
        return -(-(size // LANES) // parts) * LANES

    return share(hidden // n_sub, n_dp // 2), share(channels, n_dp // 2)


def fast(n_dp, n_sub, activations, grad_out, q_prev):
    tokens, hidden = activations.shape
    channels, rank = q_prev.shape
    block = hidden // n_sub
    width, q_width = widths(n_dp, n_sub, hidden, channels)
    padded = n_dp // 2 * width
    q_padded = n_dp // 2 * q_width
    dma = pltpu.SemaphoreType.DMA
    vmem = pl.BlockSpec(memory_space=pltpu.VMEM)
    hbm = pl.BlockSpec(memory_space=HBM)
    left, q_t = pl.pallas_call(
        functools.partial(factors_kernel, n_dp, n_sub),
        out_shape=(
            jax.ShapeDtypeStruct((3 * rank, block), BF16),
            jax.ShapeDtypeStruct((rank, q_padded), F32),
        ),
        in_specs=[hbm] * 3,
        out_specs=(vmem, vmem),
        scratch_shapes=[
            pltpu.VMEM((tokens, hidden), BF16),
            pltpu.VMEM((tokens, channels), BF16),
            pltpu.VMEM((rank, channels), BF16),
            pltpu.VMEM((n_sub - 1, rank, block), BF16),
            pltpu.VMEM((n_sub - 1, rank, block), BF16),
            pltpu.VMEM((rank, padded), F32),
            pltpu.VMEM((rank, padded), BF16),
            pltpu.VMEM((n_dp - 1, HALF, width), BF16),
            pltpu.VMEM((rank, padded), BF16),
            pltpu.VMEM((rank, padded), BF16),
            pltpu.VMEM((n_sub, rank, LANES), F32),
            pltpu.VMEM((n_sub, rank, block), BF16),
            pltpu.VMEM((rank, q_padded), F32),
            pltpu.VMEM((rank, q_padded), BF16),
            pltpu.VMEM((n_dp - 1, HALF, q_width), BF16),
            pltpu.VMEM((n_sub, HALF, q_width), F32),
            dma((2,)), dma((n_sub,)),
            dma((n_sub - 1,)), dma((n_sub - 1,)),
            dma((n_dp - 1,)), dma((n_dp - 1,)),
            dma((n_dp - 1,)), dma((n_dp - 1,)),
            dma((n_dp - 1,)), dma((n_dp - 1,)),
            dma((n_sub - 1,)), dma((n_sub - 1,)),
            dma((n_sub - 1,)), dma((n_sub - 1,)),
            dma((n_dp - 1,)), dma((n_dp - 1,)),
            dma((n_sub - 1,)), dma((n_sub - 1,)),
            dma((n_dp - 1,)), dma((n_dp - 1,)),
        ],
        compiler_params=pltpu.CompilerParams(
            collective_id=0, has_side_effects=True, vmem_limit_bytes=62 * 2**20
        ),
        name="factors",
    )(activations, grad_out, q_prev.T)
    grad, q_new = pl.pallas_call(
        result_kernel,
        out_shape=(
            jax.ShapeDtypeStruct((block, channels), F32),
            jax.ShapeDtypeStruct((rank, channels), F32),
        ),
        in_specs=[hbm, hbm],
        out_specs=(hbm, hbm),
        scratch_shapes=[
            pltpu.VMEM((3 * rank, block), BF16),
            pltpu.VMEM((rank, q_padded), F32),
            pltpu.VMEM((3 * rank, channels), BF16),
            pltpu.VMEM((block, channels), F32),
            dma((2,)),
            dma,
            dma((-(-block // ROWS),)),
        ],
        compiler_params=pltpu.CompilerParams(vmem_limit_bytes=62 * 2**20),
        name="result",
    )(left, q_t)
    return grad, q_new.T


def general(activations, grad_out, q_prev):
    u_low = jnp.dot(grad_out, q_prev, preferred_element_type=F32).astype(BF16)
    p_local = jnp.einsum("tf,tr->fr", activations, u_low, preferred_element_type=F32)
    block_rows = activations.shape[1] // lax.axis_size("sub")
    p_sum = lax.psum(p_local, ("dp", "sub"))
    gram = jnp.dot(p_sum.T, p_sum, precision=HIGHEST)
    lower = lax.linalg.cholesky(gram)
    p_hat = lax.linalg.triangular_solve(lower, p_sum, left_side=False, lower=True, transpose_a=True)
    p_low = p_hat.astype(BF16)
    my_hat = lax.dynamic_slice_in_dim(p_hat, lax.axis_index("sub") * block_rows, block_rows, 0)
    v_low = jnp.dot(activations, p_low, preferred_element_type=F32).astype(BF16)
    q_local = jnp.einsum("tc,tr->cr", grad_out, v_low, preferred_element_type=F32)
    q_sum = lax.psum(q_local, ("dp", "sub"))
    q_new = q_sum / (lax.axis_size("dp") * lax.axis_size("sub"))
    grad_approx = jnp.dot(my_hat, q_new.T, precision=HIGHEST)
    return (grad_approx, q_new)


def solution(mesh):
    n_dp, n_sub = mesh.shape["dp"], mesh.shape["sub"]

    def per_device(activations, grad_out, q_prev):
        hidden, channels, rank = activations.shape[1], grad_out.shape[1], q_prev.shape[1]
        fits = (
            n_dp % 2 == 0
            and n_sub > 1
            and rank == 2 * HALF
            and hidden % (n_sub * LANES) == 0
            and channels % LANES == 0
        )
        if fits:
            return fast(n_dp, n_sub, activations, grad_out, q_prev)
        return general(activations, grad_out, q_prev)

    return jax.shard_map(
        per_device,
        mesh=mesh,
        in_specs=(P(("dp", "sub"), None), P(("dp", "sub"), None), P()),
        out_specs=(P("sub", None), P()),
        check_vma=False,
    )
```

```python
import functools

import jax
import jax.numpy as jnp
from jax import lax
from jax.experimental import pallas as pl
from jax.experimental.pallas import tpu as pltpu
from jax.sharding import PartitionSpec as P

MESH = pl.DeviceIdType.MESH
F32 = jnp.float32
BF16 = jnp.bfloat16
HIGHEST = lax.Precision.HIGHEST
LANES = 128
HALF = 16
ROWS = 256
HBM = pltpu.MemorySpace.HBM


def dot(a, b, dims=((1,), (0,)), precision=None):
    return lax.dot_general(a, b, (dims, ((), ())), precision=precision, preferred_element_type=F32)


def inverse_factor(gram):
    rank = gram.shape[0]
    row = lax.broadcasted_iota(jnp.int32, (rank, rank), 0)
    column = lax.broadcasted_iota(jnp.int32, (rank, rank), 1)
    row2 = lax.broadcasted_iota(jnp.int32, (rank, 2 * rank), 0)
    work = jnp.concatenate([gram, jnp.where(row == column, 1.0, 0.0).astype(F32)], axis=1)
    for j in range(rank):
        scale = lax.rsqrt(work[j : j + 1, j : j + 1])
        pivot = work[j : j + 1, :] * scale
        factor = work[:, j : j + 1] * scale
        work = jnp.where(row2 > j, work - factor * pivot, jnp.where(row2 == j, pivot, work))
    return work[:, rank:]


def split(x):
    high = x.astype(BF16)
    return high, (x - high.astype(F32)).astype(BF16)


def dot_split(a, b):
    a_high, a_low = split(a)
    b_high, b_low = split(b)
    return dot(jnp.concatenate([a_high, a_high, a_low], 1), jnp.concatenate([b_high, b_low, b_high], 0))


def factors_kernel(
    n_dp, n_sub, a_hbm, g_hbm, q_hbm, left_ref, q_all,
    a_ref, g_ref, q_ref, s1_send, s1_recv, part, part_low, s2_recv, whole_high, whole_low, grams, blocks,
    q_local, q_send, qa_recv, q_parts,
    in_s, a_s, s1_s, s1_r, s2_s, s2_r, gh_s, gh_r, gl_s, gl_r, gm_s, gm_r, b_s, b_r,
    qa_s, qa_r, qb_s, qb_r, qc_s, qc_r,
):
    dp, sub = lax.axis_index("dp"), lax.axis_index("sub")
    n = n_dp * n_sub
    block = a_ref.shape[1] // n_sub
    rank, channels = q_ref.shape
    width = part.shape[1] // (n_dp // 2)
    q_width = q_all.shape[1] // (n_dp // 2)
    dp_to = [None] + [(dp + k) % n_dp for k in range(1, n_dp)]
    dp_from = [None] + [(dp + n_dp - k) % n_dp for k in range(1, n_dp)]
    chips, chip, core = n_sub // 2, sub // 2, sub % 2
    steps = [(x, c) for x in range(1, chips) for c in range(2)] + [(0, 1)]
    sub_to = [sub] + [(chip + x) % chips * 2 + (core + c) % 2 for x, c in steps]
    sub_from = [sub] + [(chip + chips - x) % chips * 2 + (core + c) % 2 for x, c in steps]

    def piece(ref, owner, wide):
        return ref.at[pl.ds(pl.multiple_of((owner % 2) * HALF, HALF), HALF),
                      pl.ds(pl.multiple_of((owner // 2) * wide, LANES), wide)]

    def columns(ref, s, wide):
        return ref.at[:, pl.ds(pl.multiple_of(s * wide, LANES), wide)]

    def send(src, dst, s, r, to):
        return pltpu.make_async_remote_copy(
            src_ref=src, dst_ref=dst, send_sem=s, recv_sem=r, device_id=to, device_id_type=MESH)

    sent = []

    def start(*copy):
        copy = send(*copy)
        copy.start()
        sent.append(copy)

    barrier = pltpu.get_barrier_semaphore()
    for k in range(1, n_sub):
        pl.semaphore_signal(barrier, inc=1, device_id=(dp, sub_to[k]), device_id_type=MESH)
    for k in range(1, n_dp):
        pl.semaphore_signal(barrier, inc=1, device_id=(dp_to[k], sub), device_id_type=MESH)

    load_g = pltpu.make_async_copy(g_hbm, g_ref, in_s.at[0])
    load_q = pltpu.make_async_copy(q_hbm, q_ref, in_s.at[1])
    load_g.start()
    load_q.start()
    loads = []
    for k in list(range(1, n_sub)) + [0]:
        load = pltpu.make_async_copy(columns(a_hbm, sub_to[k], block), columns(a_ref, sub_to[k], block), a_s.at[k])
        load.start()
        loads.append(load)
    load_g.wait()
    load_q.wait()
    u = dot(q_ref[...], g_ref[...], ((1,), (1,))).astype(BF16)
    for k in range(1, n_sub):
        loads[k - 1].wait()
        s1_send[k - 1] = dot(u, columns(a_ref, sub_to[k], block)[...]).astype(BF16)
        if k == 1:
            pl.semaphore_wait(barrier, n_sub + n_dp - 2)
        start(s1_send.at[k - 1], s1_recv.at[k - 1], s1_s.at[k - 1], s1_r.at[k - 1], (dp, sub_to[k]))
    loads[n_sub - 1].wait()
    total = dot(u, columns(a_ref, sub, block)[...])
    for k in range(1, n_sub):
        send(s1_send.at[k - 1], s1_recv.at[k - 1], s1_s.at[k - 1], s1_r.at[k - 1], (dp, sub_to[k])).wait_recv()
        total = total + s1_recv[k - 1].astype(F32)
    part[:, pl.ds(0, block)] = total
    part_low[:, pl.ds(0, block)] = total.astype(BF16)
    if part.shape[1] > block:
        rest = part.shape[1] - block
        part[:, pl.ds(block, rest)] = jnp.zeros((rank, rest), F32)
        part_low[:, pl.ds(block, rest)] = jnp.zeros((rank, rest), BF16)

    for k in range(1, n_dp):
        start(piece(part_low, dp_to[k], width), s2_recv.at[k - 1], s2_s.at[k - 1], s2_r.at[k - 1], (dp_to[k], sub))
    mine = piece(part, dp, width)[...]
    for k in range(1, n_dp):
        send(piece(part_low, dp_to[k], width), s2_recv.at[k - 1], s2_s.at[k - 1], s2_r.at[k - 1], (dp_to[k], sub)).wait_recv()
        mine = mine + s2_recv[k - 1].astype(F32)
    high, low = split(mine)
    high_piece, low_piece = piece(whole_high, dp, width), piece(whole_low, dp, width)
    high_piece[...] = high
    low_piece[...] = low
    for k in range(1, n_dp):
        start(high_piece, high_piece, gh_s.at[k - 1], gh_r.at[k - 1], (dp_to[k], sub))
    for k in range(1, n_dp):
        other = piece(whole_high, dp_from[k], width)
        send(other, other, gh_s.at[k - 1], gh_r.at[k - 1], (dp_from[k], sub)).wait_recv()

    p_high = whole_high[:, pl.ds(0, block)]
    gram = dot(p_high, p_high, ((1,), (1,)))
    grams[sub] = jnp.concatenate([gram, jnp.zeros((rank, LANES - rank), F32)], axis=1)
    for k in range(1, n_sub):
        start(grams.at[sub], grams.at[sub], gm_s.at[k - 1], gm_r.at[k - 1], (dp, sub_to[k]))
    for k in range(1, n_sub):
        start(whole_high.at[:, pl.ds(0, block)], blocks.at[sub], b_s.at[k - 1], b_r.at[k - 1], (dp, sub_to[k]))
    for k in range(1, n_dp):
        start(low_piece, low_piece, gl_s.at[k - 1], gl_r.at[k - 1], (dp_to[k], sub))
    v = dot(p_high, columns(a_ref, sub, block)[...], ((1,), (1,)))
    for k in range(1, n_sub):
        other = grams.at[sub_from[k]]
        send(other, other, gm_s.at[k - 1], gm_r.at[k - 1], (dp, sub_from[k])).wait_recv()
    gram = grams[0]
    for s in range(1, n_sub):
        gram = gram + grams[s]
    inverse = inverse_factor(gram[:, :rank])

    for k in range(n_sub - 1, 0, -1):
        other = blocks.at[sub_from[k]]
        send(other, other, b_s.at[k - 1], b_r.at[k - 1], (dp, sub_from[k])).wait_recv()
        v = v + dot(other[...], columns(a_ref, sub_from[k], block)[...], ((1,), (1,)))
    v_low = dot_split(inverse, v).astype(BF16)
    q = dot(v_low, g_ref[...])
    rest = q_all.shape[1] - channels
    if rest:
        q = jnp.concatenate([q, jnp.zeros((rank, rest), F32)], axis=1)
    q_local[...] = q
    q_send[...] = q.astype(BF16)
    for k in range(1, n_dp):
        start(piece(q_send, dp_to[k], q_width), qa_recv.at[k - 1], qa_s.at[k - 1], qa_r.at[k - 1], (dp_to[k], sub))

    for k in range(1, n_dp):
        other = piece(whole_low, dp_from[k], width)
        send(other, other, gl_s.at[k - 1], gl_r.at[k - 1], (dp_from[k], sub)).wait_recv()
    p = p_high.astype(F32) + whole_low[:, pl.ds(0, block)].astype(F32)
    high, low = split(dot_split(inverse, p))
    left_ref[pl.ds(0, rank), :] = high
    left_ref[pl.ds(rank, rank), :] = high
    left_ref[pl.ds(2 * rank, rank), :] = low

    total = piece(q_local, dp, q_width)[...]
    for k in range(1, n_dp):
        send(piece(q_send, dp_to[k], q_width), qa_recv.at[k - 1], qa_s.at[k - 1], qa_r.at[k - 1], (dp_to[k], sub)).wait_recv()
        total = total + qa_recv[k - 1].astype(F32)
    q_parts[sub] = total
    for k in range(1, n_sub):
        start(q_parts.at[sub], q_parts.at[sub], qb_s.at[k - 1], qb_r.at[k - 1], (dp, sub_to[k]))
    for k in range(1, n_sub):
        other = q_parts.at[sub_from[k]]
        send(other, other, qb_s.at[k - 1], qb_r.at[k - 1], (dp, sub_from[k])).wait_recv()
    total = q_parts[0]
    for s in range(1, n_sub):
        total = total + q_parts[s]
    mine = piece(q_all, dp, q_width)
    mine[...] = total * (1.0 / n)
    for k in range(1, n_dp):
        start(mine, mine, qc_s.at[k - 1], qc_r.at[k - 1], (dp_to[k], sub))
    for k in range(1, n_dp):
        other = piece(q_all, dp_from[k], q_width)
        send(other, other, qc_s.at[k - 1], qc_r.at[k - 1], (dp_from[k], sub)).wait_recv()

    for copy in sent:
        copy.wait_send()


def result_kernel(left_hbm, q_hbm, grad_ref, q_new_ref, left_ref, q_ref, right, held, in_s, q_s, out_s):
    rank, channels = q_new_ref.shape
    load_q = pltpu.make_async_copy(q_hbm, q_ref, in_s.at[0])
    load_left = pltpu.make_async_copy(left_hbm, left_ref, in_s.at[1])
    load_q.start()
    load_left.start()
    load_q.wait()
    copies = [pltpu.make_async_copy(q_ref.at[:, pl.ds(0, channels)], q_new_ref, q_s)]
    copies[0].start()
    high, low = split(q_ref[:, pl.ds(0, channels)])
    right[pl.ds(0, rank), :] = high
    right[pl.ds(rank, rank), :] = low
    right[pl.ds(2 * rank, rank), :] = high
    load_left.wait()
    rows = grad_ref.shape[0]
    edges = [0] + list(range(LANES, rows, ROWS)) + [rows]
    for i, (at, end) in enumerate(zip(edges, edges[1:])):
        here = pl.ds(at, end - at)
        held[here, :] = dot(left_ref[:, here], right[...], ((0,), (0,)))
        copies.append(pltpu.make_async_copy(held.at[here], grad_ref.at[here], out_s.at[i]))
        copies[-1].start()
    for copy in copies:
        copy.wait()


def widths(n_dp, n_sub, hidden, channels):
    def share(size, parts):
        return -(-(size // LANES) // parts) * LANES

    return share(hidden // n_sub, n_dp // 2), share(channels, n_dp // 2)


def fast(n_dp, n_sub, activations, grad_out, q_prev):
    tokens, hidden = activations.shape
    channels, rank = q_prev.shape
    block = hidden // n_sub
    width, q_width = widths(n_dp, n_sub, hidden, channels)
    padded = n_dp // 2 * width
    q_padded = n_dp // 2 * q_width
    dma = pltpu.SemaphoreType.DMA
    vmem = pl.BlockSpec(memory_space=pltpu.VMEM)
    hbm = pl.BlockSpec(memory_space=HBM)
    left, q_t = pl.pallas_call(
        functools.partial(factors_kernel, n_dp, n_sub),
        out_shape=(
            jax.ShapeDtypeStruct((3 * rank, block), BF16),
            jax.ShapeDtypeStruct((rank, q_padded), F32),
        ),
        in_specs=[hbm] * 3,
        out_specs=(vmem, vmem),
        scratch_shapes=[
            pltpu.VMEM((tokens, hidden), BF16),
            pltpu.VMEM((tokens, channels), BF16),
            pltpu.VMEM((rank, channels), BF16),
            pltpu.VMEM((n_sub - 1, rank, block), BF16),
            pltpu.VMEM((n_sub - 1, rank, block), BF16),
            pltpu.VMEM((rank, padded), F32),
            pltpu.VMEM((rank, padded), BF16),
            pltpu.VMEM((n_dp - 1, HALF, width), BF16),
            pltpu.VMEM((rank, padded), BF16),
            pltpu.VMEM((rank, padded), BF16),
            pltpu.VMEM((n_sub, rank, LANES), F32),
            pltpu.VMEM((n_sub, rank, block), BF16),
            pltpu.VMEM((rank, q_padded), F32),
            pltpu.VMEM((rank, q_padded), BF16),
            pltpu.VMEM((n_dp - 1, HALF, q_width), BF16),
            pltpu.VMEM((n_sub, HALF, q_width), F32),
            dma((2,)), dma((n_sub,)),
            dma((n_sub - 1,)), dma((n_sub - 1,)),
            dma((n_dp - 1,)), dma((n_dp - 1,)),
            dma((n_dp - 1,)), dma((n_dp - 1,)),
            dma((n_dp - 1,)), dma((n_dp - 1,)),
            dma((n_sub - 1,)), dma((n_sub - 1,)),
            dma((n_sub - 1,)), dma((n_sub - 1,)),
            dma((n_dp - 1,)), dma((n_dp - 1,)),
            dma((n_sub - 1,)), dma((n_sub - 1,)),
            dma((n_dp - 1,)), dma((n_dp - 1,)),
        ],
        compiler_params=pltpu.CompilerParams(
            collective_id=0, has_side_effects=True, vmem_limit_bytes=62 * 2**20
        ),
        name="factors",
    )(activations, grad_out, q_prev.T)
    grad, q_new = pl.pallas_call(
        result_kernel,
        out_shape=(
            jax.ShapeDtypeStruct((block, channels), F32),
            jax.ShapeDtypeStruct((rank, channels), F32),
        ),
        in_specs=[hbm, hbm],
        out_specs=(hbm, hbm),
        scratch_shapes=[
            pltpu.VMEM((3 * rank, block), BF16),
            pltpu.VMEM((rank, q_padded), F32),
            pltpu.VMEM((3 * rank, channels), BF16),
            pltpu.VMEM((block, channels), F32),
            dma((2,)),
            dma,
            dma((1 + -(-block // ROWS),)),
        ],
        compiler_params=pltpu.CompilerParams(vmem_limit_bytes=62 * 2**20),
        name="result",
    )(left, q_t)
    return grad, q_new.T


def general(activations, grad_out, q_prev):
    u_low = jnp.dot(grad_out, q_prev, preferred_element_type=F32).astype(BF16)
    p_local = jnp.einsum("tf,tr->fr", activations, u_low, preferred_element_type=F32)
    block_rows = activations.shape[1] // lax.axis_size("sub")
    p_sum = lax.psum(p_local, ("dp", "sub"))
    gram = jnp.dot(p_sum.T, p_sum, precision=HIGHEST)
    lower = lax.linalg.cholesky(gram)
    p_hat = lax.linalg.triangular_solve(lower, p_sum, left_side=False, lower=True, transpose_a=True)
    p_low = p_hat.astype(BF16)
    my_hat = lax.dynamic_slice_in_dim(p_hat, lax.axis_index("sub") * block_rows, block_rows, 0)
    v_low = jnp.dot(activations, p_low, preferred_element_type=F32).astype(BF16)
    q_local = jnp.einsum("tc,tr->cr", grad_out, v_low, preferred_element_type=F32)
    q_sum = lax.psum(q_local, ("dp", "sub"))
    q_new = q_sum / (lax.axis_size("dp") * lax.axis_size("sub"))
    grad_approx = jnp.dot(my_hat, q_new.T, precision=HIGHEST)
    return (grad_approx, q_new)


def solution(mesh):
    n_dp, n_sub = mesh.shape["dp"], mesh.shape["sub"]

    def per_device(activations, grad_out, q_prev):
        hidden, channels, rank = activations.shape[1], grad_out.shape[1], q_prev.shape[1]
        fits = (
            n_dp % 2 == 0
            and n_sub % 2 == 0
            and rank == 2 * HALF
            and hidden % (n_sub * LANES) == 0
            and channels % LANES == 0
        )
        if fits:
            return fast(n_dp, n_sub, activations, grad_out, q_prev)
        return general(activations, grad_out, q_prev)

    return jax.shard_map(
        per_device,
        mesh=mesh,
        in_specs=(P(("dp", "sub"), None), P(("dp", "sub"), None), P()),
        out_specs=(P("sub", None), P()),
        check_vma=False,
    )
```

```python
import functools

import jax
import jax.numpy as jnp
from jax import lax
from jax.experimental import pallas as pl
from jax.experimental.pallas import tpu as pltpu
from jax.sharding import PartitionSpec as P

MESH = pl.DeviceIdType.MESH
F32 = jnp.float32
BF16 = jnp.bfloat16
HIGHEST = lax.Precision.HIGHEST
LANES = 128
HALF = 16
ROWS = 256
HBM = pltpu.MemorySpace.HBM


def dot(a, b, dims=((1,), (0,)), precision=None):
    return lax.dot_general(a, b, (dims, ((), ())), precision=precision, preferred_element_type=F32)


def inverse_factor(gram):
    rank = gram.shape[0]
    row = lax.broadcasted_iota(jnp.int32, (rank, rank), 0)
    column = lax.broadcasted_iota(jnp.int32, (rank, rank), 1)
    row2 = lax.broadcasted_iota(jnp.int32, (rank, 2 * rank), 0)
    work = jnp.concatenate([gram, jnp.where(row == column, 1.0, 0.0).astype(F32)], axis=1)
    for j in range(rank):
        scale = lax.rsqrt(work[j : j + 1, j : j + 1])
        pivot = work[j : j + 1, :] * scale
        factor = work[:, j : j + 1] * scale
        work = jnp.where(row2 > j, work - factor * pivot, jnp.where(row2 == j, pivot, work))
    return work[:, rank:]


def split(x):
    high = x.astype(BF16)
    return high, (x - high.astype(F32)).astype(BF16)


def dot_split(a, b):
    a_high, a_low = split(a)
    b_high, b_low = split(b)
    return dot(jnp.concatenate([a_high, a_high, a_low], 1), jnp.concatenate([b_high, b_low, b_high], 0))


def factors_kernel(
    n_dp, n_sub, a_hbm, g_hbm, q_hbm, left_ref, q_all,
    a_ref, g_ref, q_ref, s1_send, s1_recv, part, part_low, s2_recv, whole_high, whole_low, grams, blocks,
    q_local, q_send, qa_recv, q_parts,
    in_s, a_s, s1_s, s1_r, s2_s, s2_r, gh_s, gh_r, gl_s, gl_r, gm_s, gm_r, b_s, b_r,
    qa_s, qa_r, qb_s, qb_r, qc_s, qc_r,
):
    dp, sub = lax.axis_index("dp"), lax.axis_index("sub")
    n = n_dp * n_sub
    block = a_ref.shape[1] // n_sub
    rank, channels = q_ref.shape
    width = part.shape[1] // (n_dp // 2)
    q_width = q_all.shape[1] // (n_dp // 2)
    far_first = sorted(range(1, n_dp), key=lambda k: -min(k, n_dp - k))
    dp_to = [None] + [(dp + k) % n_dp for k in far_first]
    dp_from = [None] + [(dp + n_dp - k) % n_dp for k in far_first]
    chips, chip, core = n_sub // 2, sub // 2, sub % 2
    steps = [(x, c) for x in range(1, chips) for c in range(2)] + [(0, 1)]
    sub_to = [sub] + [(chip + x) % chips * 2 + (core + c) % 2 for x, c in steps]
    sub_from = [sub] + [(chip + chips - x) % chips * 2 + (core + c) % 2 for x, c in steps]

    def piece(ref, owner, wide):
        return ref.at[pl.ds(pl.multiple_of((owner % 2) * HALF, HALF), HALF),
                      pl.ds(pl.multiple_of((owner // 2) * wide, LANES), wide)]

    def columns(ref, s, wide):
        return ref.at[:, pl.ds(pl.multiple_of(s * wide, LANES), wide)]

    def send(src, dst, s, r, to):
        return pltpu.make_async_remote_copy(
            src_ref=src, dst_ref=dst, send_sem=s, recv_sem=r, device_id=to, device_id_type=MESH)

    sent = []

    def start(*copy):
        copy = send(*copy)
        copy.start()
        sent.append(copy)

    barrier = pltpu.get_barrier_semaphore()
    for k in range(1, n_sub):
        pl.semaphore_signal(barrier, inc=1, device_id=(dp, sub_to[k]), device_id_type=MESH)
    for k in range(1, n_dp):
        pl.semaphore_signal(barrier, inc=1, device_id=(dp_to[k], sub), device_id_type=MESH)

    load_g = pltpu.make_async_copy(g_hbm, g_ref, in_s.at[0])
    load_q = pltpu.make_async_copy(q_hbm, q_ref, in_s.at[1])
    load_g.start()
    load_q.start()
    loads = []
    for k in list(range(1, n_sub)) + [0]:
        load = pltpu.make_async_copy(columns(a_hbm, sub_to[k], block), columns(a_ref, sub_to[k], block), a_s.at[k])
        load.start()
        loads.append(load)
    load_g.wait()
    load_q.wait()
    u = dot(q_ref[...], g_ref[...], ((1,), (1,))).astype(BF16)
    for k in range(1, n_sub):
        loads[k - 1].wait()
        s1_send[k - 1] = dot(u, columns(a_ref, sub_to[k], block)[...]).astype(BF16)
        if k == 1:
            pl.semaphore_wait(barrier, n_sub + n_dp - 2)
        start(s1_send.at[k - 1], s1_recv.at[k - 1], s1_s.at[k - 1], s1_r.at[k - 1], (dp, sub_to[k]))
    loads[n_sub - 1].wait()
    total = dot(u, columns(a_ref, sub, block)[...])
    for k in range(1, n_sub):
        send(s1_send.at[k - 1], s1_recv.at[k - 1], s1_s.at[k - 1], s1_r.at[k - 1], (dp, sub_to[k])).wait_recv()
        total = total + s1_recv[k - 1].astype(F32)
    part[:, pl.ds(0, block)] = total
    part_low[:, pl.ds(0, block)] = total.astype(BF16)
    if part.shape[1] > block:
        rest = part.shape[1] - block
        part[:, pl.ds(block, rest)] = jnp.zeros((rank, rest), F32)
        part_low[:, pl.ds(block, rest)] = jnp.zeros((rank, rest), BF16)

    for k in range(1, n_dp):
        start(piece(part_low, dp_to[k], width), s2_recv.at[k - 1], s2_s.at[k - 1], s2_r.at[k - 1], (dp_to[k], sub))
    mine = piece(part, dp, width)[...]
    for k in range(1, n_dp):
        send(piece(part_low, dp_to[k], width), s2_recv.at[k - 1], s2_s.at[k - 1], s2_r.at[k - 1], (dp_to[k], sub)).wait_recv()
        mine = mine + s2_recv[k - 1].astype(F32)
    high, low = split(mine)
    high_piece, low_piece = piece(whole_high, dp, width), piece(whole_low, dp, width)
    high_piece[...] = high
    low_piece[...] = low
    for k in range(1, n_dp):
        start(high_piece, high_piece, gh_s.at[k - 1], gh_r.at[k - 1], (dp_to[k], sub))
    for k in range(1, n_dp):
        other = piece(whole_high, dp_from[k], width)
        send(other, other, gh_s.at[k - 1], gh_r.at[k - 1], (dp_from[k], sub)).wait_recv()

    p_high = whole_high[:, pl.ds(0, block)]
    gram = dot(p_high, p_high, ((1,), (1,)))
    grams[sub] = jnp.concatenate([gram, jnp.zeros((rank, LANES - rank), F32)], axis=1)
    for k in range(1, n_sub):
        start(grams.at[sub], grams.at[sub], gm_s.at[k - 1], gm_r.at[k - 1], (dp, sub_to[k]))
    for k in range(1, n_sub):
        start(whole_high.at[:, pl.ds(0, block)], blocks.at[sub], b_s.at[k - 1], b_r.at[k - 1], (dp, sub_to[k]))
    for k in range(1, n_dp):
        start(low_piece, low_piece, gl_s.at[k - 1], gl_r.at[k - 1], (dp_to[k], sub))
    v = dot(p_high, columns(a_ref, sub, block)[...], ((1,), (1,)))
    for k in range(1, n_sub):
        other = grams.at[sub_from[k]]
        send(other, other, gm_s.at[k - 1], gm_r.at[k - 1], (dp, sub_from[k])).wait_recv()
    gram = grams[0]
    for s in range(1, n_sub):
        gram = gram + grams[s]
    inverse = inverse_factor(gram[:, :rank])

    for k in range(n_sub - 1, 0, -1):
        other = blocks.at[sub_from[k]]
        send(other, other, b_s.at[k - 1], b_r.at[k - 1], (dp, sub_from[k])).wait_recv()
        v = v + dot(other[...], columns(a_ref, sub_from[k], block)[...], ((1,), (1,)))
    v_low = dot_split(inverse, v).astype(BF16)
    q = dot(v_low, g_ref[...])
    rest = q_all.shape[1] - channels
    if rest:
        q = jnp.concatenate([q, jnp.zeros((rank, rest), F32)], axis=1)
    q_local[...] = q
    q_send[...] = q.astype(BF16)
    for k in range(1, n_dp):
        start(piece(q_send, dp_to[k], q_width), qa_recv.at[k - 1], qa_s.at[k - 1], qa_r.at[k - 1], (dp_to[k], sub))

    for k in range(1, n_dp):
        other = piece(whole_low, dp_from[k], width)
        send(other, other, gl_s.at[k - 1], gl_r.at[k - 1], (dp_from[k], sub)).wait_recv()
    p = p_high.astype(F32) + whole_low[:, pl.ds(0, block)].astype(F32)
    high, low = split(dot_split(inverse, p))
    left_ref[pl.ds(0, rank), :] = high
    left_ref[pl.ds(rank, rank), :] = high
    left_ref[pl.ds(2 * rank, rank), :] = low

    total = piece(q_local, dp, q_width)[...]
    for k in range(1, n_dp):
        send(piece(q_send, dp_to[k], q_width), qa_recv.at[k - 1], qa_s.at[k - 1], qa_r.at[k - 1], (dp_to[k], sub)).wait_recv()
        total = total + qa_recv[k - 1].astype(F32)
    q_parts[sub] = total
    for k in range(1, n_sub):
        start(q_parts.at[sub], q_parts.at[sub], qb_s.at[k - 1], qb_r.at[k - 1], (dp, sub_to[k]))
    for k in range(1, n_sub):
        other = q_parts.at[sub_from[k]]
        send(other, other, qb_s.at[k - 1], qb_r.at[k - 1], (dp, sub_from[k])).wait_recv()
    total = q_parts[0]
    for s in range(1, n_sub):
        total = total + q_parts[s]
    mine = piece(q_all, dp, q_width)
    mine[...] = total * (1.0 / n)
    for k in range(1, n_dp):
        start(mine, mine, qc_s.at[k - 1], qc_r.at[k - 1], (dp_to[k], sub))
    for k in range(1, n_dp):
        other = piece(q_all, dp_from[k], q_width)
        send(other, other, qc_s.at[k - 1], qc_r.at[k - 1], (dp_from[k], sub)).wait_recv()

    for copy in sent:
        copy.wait_send()


def result_kernel(left_hbm, q_hbm, grad_ref, q_new_ref, left_ref, q_ref, right, held, in_s, q_s, out_s):
    rank, channels = q_new_ref.shape
    load_q = pltpu.make_async_copy(q_hbm, q_ref, in_s.at[0])
    load_left = pltpu.make_async_copy(left_hbm, left_ref, in_s.at[1])
    load_q.start()
    load_left.start()
    load_q.wait()
    copies = [pltpu.make_async_copy(q_ref.at[:, pl.ds(0, channels)], q_new_ref, q_s)]
    copies[0].start()
    high, low = split(q_ref[:, pl.ds(0, channels)])
    right[pl.ds(0, rank), :] = high
    right[pl.ds(rank, rank), :] = low
    right[pl.ds(2 * rank, rank), :] = high
    load_left.wait()
    rows = grad_ref.shape[0]
    edges = [0] + list(range(LANES, rows, ROWS)) + [rows]
    for i, (at, end) in enumerate(zip(edges, edges[1:])):
        here = pl.ds(at, end - at)
        held[here, :] = dot(left_ref[:, here], right[...], ((0,), (0,)))
        copies.append(pltpu.make_async_copy(held.at[here], grad_ref.at[here], out_s.at[i]))
        copies[-1].start()
    for copy in copies:
        copy.wait()


def widths(n_dp, n_sub, hidden, channels):
    def share(size, parts):
        return -(-(size // LANES) // parts) * LANES

    return share(hidden // n_sub, n_dp // 2), share(channels, n_dp // 2)


def fast(n_dp, n_sub, activations, grad_out, q_prev):
    tokens, hidden = activations.shape
    channels, rank = q_prev.shape
    block = hidden // n_sub
    width, q_width = widths(n_dp, n_sub, hidden, channels)
    padded = n_dp // 2 * width
    q_padded = n_dp // 2 * q_width
    dma = pltpu.SemaphoreType.DMA
    vmem = pl.BlockSpec(memory_space=pltpu.VMEM)
    hbm = pl.BlockSpec(memory_space=HBM)
    left, q_t = pl.pallas_call(
        functools.partial(factors_kernel, n_dp, n_sub),
        out_shape=(
            jax.ShapeDtypeStruct((3 * rank, block), BF16),
            jax.ShapeDtypeStruct((rank, q_padded), F32),
        ),
        in_specs=[hbm] * 3,
        out_specs=(vmem, vmem),
        scratch_shapes=[
            pltpu.VMEM((tokens, hidden), BF16),
            pltpu.VMEM((tokens, channels), BF16),
            pltpu.VMEM((rank, channels), BF16),
            pltpu.VMEM((n_sub - 1, rank, block), BF16),
            pltpu.VMEM((n_sub - 1, rank, block), BF16),
            pltpu.VMEM((rank, padded), F32),
            pltpu.VMEM((rank, padded), BF16),
            pltpu.VMEM((n_dp - 1, HALF, width), BF16),
            pltpu.VMEM((rank, padded), BF16),
            pltpu.VMEM((rank, padded), BF16),
            pltpu.VMEM((n_sub, rank, LANES), F32),
            pltpu.VMEM((n_sub, rank, block), BF16),
            pltpu.VMEM((rank, q_padded), F32),
            pltpu.VMEM((rank, q_padded), BF16),
            pltpu.VMEM((n_dp - 1, HALF, q_width), BF16),
            pltpu.VMEM((n_sub, HALF, q_width), F32),
            dma((2,)), dma((n_sub,)),
            dma((n_sub - 1,)), dma((n_sub - 1,)),
            dma((n_dp - 1,)), dma((n_dp - 1,)),
            dma((n_dp - 1,)), dma((n_dp - 1,)),
            dma((n_dp - 1,)), dma((n_dp - 1,)),
            dma((n_sub - 1,)), dma((n_sub - 1,)),
            dma((n_sub - 1,)), dma((n_sub - 1,)),
            dma((n_dp - 1,)), dma((n_dp - 1,)),
            dma((n_sub - 1,)), dma((n_sub - 1,)),
            dma((n_dp - 1,)), dma((n_dp - 1,)),
        ],
        compiler_params=pltpu.CompilerParams(
            collective_id=0, has_side_effects=True, vmem_limit_bytes=62 * 2**20
        ),
        name="factors",
    )(activations, grad_out, q_prev.T)
    grad, q_new = pl.pallas_call(
        result_kernel,
        out_shape=(
            jax.ShapeDtypeStruct((block, channels), F32),
            jax.ShapeDtypeStruct((rank, channels), F32),
        ),
        in_specs=[hbm, hbm],
        out_specs=(hbm, hbm),
        scratch_shapes=[
            pltpu.VMEM((3 * rank, block), BF16),
            pltpu.VMEM((rank, q_padded), F32),
            pltpu.VMEM((3 * rank, channels), BF16),
            pltpu.VMEM((block, channels), F32),
            dma((2,)),
            dma,
            dma((1 + -(-block // ROWS),)),
        ],
        compiler_params=pltpu.CompilerParams(vmem_limit_bytes=62 * 2**20),
        name="result",
    )(left, q_t)
    return grad, q_new.T


def general(activations, grad_out, q_prev):
    u_low = jnp.dot(grad_out, q_prev, preferred_element_type=F32).astype(BF16)
    p_local = jnp.einsum("tf,tr->fr", activations, u_low, preferred_element_type=F32)
    block_rows = activations.shape[1] // lax.axis_size("sub")
    p_sum = lax.psum(p_local, ("dp", "sub"))
    gram = jnp.dot(p_sum.T, p_sum, precision=HIGHEST)
    lower = lax.linalg.cholesky(gram)
    p_hat = lax.linalg.triangular_solve(lower, p_sum, left_side=False, lower=True, transpose_a=True)
    p_low = p_hat.astype(BF16)
    my_hat = lax.dynamic_slice_in_dim(p_hat, lax.axis_index("sub") * block_rows, block_rows, 0)
    v_low = jnp.dot(activations, p_low, preferred_element_type=F32).astype(BF16)
    q_local = jnp.einsum("tc,tr->cr", grad_out, v_low, preferred_element_type=F32)
    q_sum = lax.psum(q_local, ("dp", "sub"))
    q_new = q_sum / (lax.axis_size("dp") * lax.axis_size("sub"))
    grad_approx = jnp.dot(my_hat, q_new.T, precision=HIGHEST)
    return (grad_approx, q_new)


def solution(mesh):
    n_dp, n_sub = mesh.shape["dp"], mesh.shape["sub"]

    def per_device(activations, grad_out, q_prev):
        hidden, channels, rank = activations.shape[1], grad_out.shape[1], q_prev.shape[1]
        fits = (
            n_dp % 2 == 0
            and n_sub % 2 == 0
            and rank == 2 * HALF
            and hidden % (n_sub * LANES) == 0
            and channels % LANES == 0
        )
        if fits:
            return fast(n_dp, n_sub, activations, grad_out, q_prev)
        return general(activations, grad_out, q_prev)

    return jax.shard_map(
        per_device,
        mesh=mesh,
        in_specs=(P(("dp", "sub"), None), P(("dp", "sub"), None), P()),
        out_specs=(P("sub", None), P()),
        check_vma=False,
    )
```
